32 devices in a mesh: blk: 8 (over z, y), grp: 4 (over x, core).
Axes of the slice: x: 2, y: 2, z: 4, core: 2. Of those that a mesh axis runs over, the one named last changes fastest.
Arguments:
- block_inverse: bfloat16 [64, 1024, 1024], P(('blk', 'grp')), may hold values from -5 to 5
- coupling_in: bfloat16 [64, 1024, 1536], P(('blk', 'grp')), may hold values from -0.046875 to 0.046875
- coupling_out: bfloat16 [64, 1536, 1024], P(('blk', 'grp')), may hold values from -0.15625 to 0.15625
- sensitivities: bfloat16 [64, 1024, 512], P(('blk', 'grp')), may hold values from -6 to 6
- border_rhs: bfloat16 [1536, 512], replicated, may hold values from -6 to 6
- border_inverse: bfloat16 [1536, 1536], P('blk'), may hold values from -5 to 5
Outputs:
- adjoint: bfloat16 [64, 1024, 512], P(('blk', 'grp'))
- border_part: bfloat16 [1536, 512], P('blk')
The draws below stay inside these ranges and needn't reach their ends.
All inputs are finite; a program needn't handle non-finite values.
Results may differ from the reference program's by a relative error of at most 0.0067.
Values may be sent and summed in bfloat16 or wider, within the bound.
A program may use at most 128 MiB of HBM per device.

```python
import math
import jax
import jax.numpy as jnp
from jax import lax

BLOCK = 1024
LINK = 1536
COLS = 512
NBLOCKS = 64


def dominant_matrix(key, lead_shape, order):
    key_diag, key_off = jax.random.split(key, 2)
    diag_vals = jax.random.uniform(key_diag, lead_shape + (order,), jnp.float32, 0.5, 1.5)
    off_vals = jnp.clip(jax.random.normal(key_off, lead_shape + (order, order), jnp.float32), -4.0, 4.0) * (0.5 / math.sqrt(order))
    matrix = off_vals + jnp.eye(order, dtype=jnp.float32) * diag_vals[..., None, :]
    return matrix


def draw_block_inverse(key, part):
    return dominant_matrix(jax.random.fold_in(key, 11), (NBLOCKS,), BLOCK).astype(jnp.bfloat16)


def draw_border_inverse(key, part):
    return dominant_matrix(jax.random.fold_in(key, 23), (), LINK).astype(jnp.bfloat16)


def spiked(values, key, source, target, shards_of, factor):
    def block_of(dim):
        return (jnp.arange(values.shape[dim]) // (values.shape[dim] // shards_of)).reshape((-1,) + (1,) * (values.ndim - 1 - dim))

    one_side = jax.random.permutation(key, shards_of)[block_of(target)]
    other_side = (block_of(target) + shards_of // 2) % shards_of
    return jnp.where((block_of(source) == one_side) | (block_of(source) == other_side), factor * values, values)


def level_of(own_key, shape, pieces, smallest, largest):
    def one(dim, blocks):
        draws = jax.random.uniform(jax.random.fold_in(jax.random.fold_in(own_key, 6), dim), (blocks,), jnp.float32, smallest / len(pieces), largest / len(pieces))
        return jnp.repeat(jnp.exp(draws), shape[dim] // blocks).reshape((-1,) + (1,) * (len(shape) - dim - 1))

    gain = one(*pieces[0])
    for cut in pieces[1:]:
        gain = gain * one(*cut)
    return gain


def centred(key, shape, deviation, bound, cuts=(), kind=jnp.bfloat16):
    level = level_of(key, shape, cuts, -0.22, 0.18) if cuts else 1.0
    array = jax.random.normal(key, shape, jnp.float32) * deviation * level
    return jnp.minimum(jnp.maximum(array, -bound), bound).astype(kind)


def noise_with(key, shape, spread, limit, shards, heavy, kind=jnp.bfloat16):
    result = spread * jax.random.normal(key, shape, jnp.float32)
    if shards:
        result = result * level_of(key, shape, shards, -0.22, 0.18)
    return jnp.clip(spiked(result, jax.random.fold_in(key, 3), *heavy), -limit, limit).astype(kind)


def setup_inputs(seed: int = 0) -> dict:
    key_list = jax.random.split(jax.random.key(seed), 7)
    block_inverse = draw_block_inverse(jax.random.fold_in(key_list[6], 71), 0)
    coupling_in = noise_with(key_list[1], (NBLOCKS, BLOCK, LINK), (BLOCK * NBLOCKS) ** -0.5, 0.046875, ((0, 32),), (0, 2, 32, 2.75))
    coupling_out = centred(key_list[2], (NBLOCKS, LINK, BLOCK), LINK ** -0.5, 0.15625, ((0, 32),))
    sensitivities = centred(key_list[3], (NBLOCKS, BLOCK, COLS), 1.0, 6.0, ((0, 32),))
    border_rhs = centred(key_list[4], (LINK, COLS), 1.0, 6.0)
    border_inverse = draw_border_inverse(jax.random.fold_in(key_list[6], 71), 0)
    return dict(block_inverse=block_inverse, coupling_in=coupling_in, coupling_out=coupling_out, sensitivities=sensitivities, border_rhs=border_rhs, border_inverse=border_inverse)


def reference(block_inverse, coupling_in, coupling_out, sensitivities, border_rhs, border_inverse):
    def first_pass(running, blocks):
        inverse_block, couple_block, sens_block = blocks
        forward_block = jnp.dot(inverse_block.T, sens_block, preferred_element_type=jnp.float32)
        forward_half = forward_block.astype(jnp.bfloat16)
        running = running + jnp.dot(couple_block.T, forward_half, preferred_element_type=jnp.float32)
        return running, forward_block

    start_sum = jnp.zeros((LINK, COLS), jnp.float32)
    summed, forward_part = lax.scan(first_pass, start_sum, (block_inverse, coupling_in, sensitivities))
    residual = border_rhs.astype(jnp.float32) - summed
    residual_half = residual.astype(jnp.bfloat16)
    border_part = jnp.dot(border_inverse.T, residual_half, preferred_element_type=jnp.float32).astype(jnp.bfloat16)

    def second_pass(blocks):
        inverse_block, couple_block, forward_block = blocks
        pulled = jnp.dot(couple_block.T, border_part, preferred_element_type=jnp.float32).astype(jnp.bfloat16)
        back_term = jnp.dot(inverse_block.T, pulled, preferred_element_type=jnp.float32)
        return (forward_block - back_term).astype(jnp.bfloat16)

    adjoint = lax.map(second_pass, (block_inverse, coupling_out, forward_part))
    return adjoint, border_part
```

```python
import functools

import jax
import jax.numpy as jnp
from jax import lax
from jax.experimental import pallas as pl
from jax.experimental.pallas import tpu as pltpu
from jax.sharding import PartitionSpec as P

MESH = pl.DeviceIdType.MESH


def bit_of(index, k):
    return lax.rem(lax.div(index, 1 << k), 2)


def partner_of(index, k):
    return index + (1 - 2 * bit_of(index, k)) * (1 << k)


def border_kernel(
    n_blk, n_grp, term_ref, rhs_ref, inv_ref, out_ref,
    fold_refs, land_refs, sum_slots, part_ref, part_slots,
    fold_send, fold_recv, sum_send, sum_recv, part_send, part_recv,
    rows_send, rows_recv, cols_send, cols_recv,
):
    b = lax.axis_index("blk")
    g = lax.axis_index("grp")
    link, cols = term_ref.shape
    rows = link // n_blk
    steps = n_grp.bit_length() - 1
    f32 = jnp.float32

    barrier = pltpu.get_barrier_semaphore()
    for k in range(steps):
        pl.semaphore_signal(barrier, inc=1, device_id=(b, partner_of(g, k)), device_id_type=MESH)
    for d in range(1, n_blk):
        pl.semaphore_signal(barrier, inc=1, device_id=(lax.rem(b + d, n_blk), g), device_id_type=MESH)
    pl.semaphore_wait(barrier, steps + n_blk - 1)

    def row_block(index):
        return pl.ds(pl.multiple_of(index * rows, rows), rows)

    source = term_ref
    base = 0
    bases = []
    for k in range(steps):
        half = cols >> (k + 1)
        bit = bit_of(g, k)
        keep = pl.ds(pl.multiple_of(bit * half, half), half)
        give = pl.ds(pl.multiple_of((1 - bit) * half, half), half)
        copy = pltpu.make_async_remote_copy(
            src_ref=source.at[:, give], dst_ref=land_refs[k],
            send_sem=fold_send.at[k], recv_sem=fold_recv.at[k],
            device_id=(b, partner_of(g, k)), device_id_type=MESH,
        )
        copy.start()
        copy.wait()
        fold_refs[k][...] = (
            source[:, keep].astype(f32) + land_refs[k][...].astype(f32)
        ).astype(jnp.bfloat16)
        bases.append(base)
        base = base + bit * half
        source = fold_refs[k]

    def scatter(src, slots, send, recv):
        copies = []
        for d in range(1, n_blk):
            peer = lax.rem(b + d, n_blk)
            copy = pltpu.make_async_remote_copy(
                src_ref=src.at[row_block(peer), :], dst_ref=slots.at[d - 1],
                send_sem=send.at[d - 1], recv_sem=recv.at[d - 1],
                device_id=(peer, g), device_id_type=MESH,
            )
            copy.start()
            copies.append(copy)
        total = src[row_block(b), :].astype(f32)
        for d in range(1, n_blk):
            copies[d - 1].wait()
            total = total + slots[d - 1].astype(f32)
        return total

    residual = rhs_ref[...].astype(f32) - scatter(source, sum_slots, sum_send, sum_recv)
    part_ref[...] = lax.dot_general(
        inv_ref[...], residual.astype(jnp.bfloat16),
        (((0,), (0,)), ((), ())), preferred_element_type=f32,
    ).astype(jnp.bfloat16)
    width = cols // n_grp
    mine = scatter(part_ref, part_slots, part_send, part_recv)
    own_cols = pl.ds(pl.multiple_of(base, width), width)
    out_ref[row_block(b), own_cols] = mine.astype(jnp.bfloat16)

    copies = []
    for d in range(1, n_blk):
        place = out_ref.at[row_block(b), own_cols]
        copy = pltpu.make_async_remote_copy(
            src_ref=place, dst_ref=place,
            send_sem=rows_send.at[d - 1], recv_sem=rows_recv.at[d - 1],
            device_id=(lax.rem(b + d, n_blk), g), device_id_type=MESH,
        )
        copy.start()
        copies.append(copy)
    for d in range(1, n_blk):
        place = out_ref.at[row_block(lax.rem(b + n_blk - d, n_blk)), own_cols]
        copies[d - 1].wait_send()
        pltpu.make_async_remote_copy(
            src_ref=place, dst_ref=place,
            send_sem=rows_send.at[d - 1], recv_sem=rows_recv.at[d - 1],
            device_id=(lax.rem(b + d, n_blk), g), device_id_type=MESH,
        ).wait_recv()
    for k in reversed(range(steps)):
        half = cols >> (k + 1)
        bit = bit_of(g, k)
        place = out_ref.at[:, pl.ds(pl.multiple_of(bases[k] + bit * half, half), half)]
        other = out_ref.at[:, pl.ds(pl.multiple_of(bases[k] + (1 - bit) * half, half), half)]
        copy = pltpu.make_async_remote_copy(
            src_ref=place, dst_ref=place,
            send_sem=cols_send.at[k], recv_sem=cols_recv.at[k],
            device_id=(b, partner_of(g, k)), device_id_type=MESH,
        )
        copy.start()
        copy.wait_send()
        pltpu.make_async_remote_copy(
            src_ref=other, dst_ref=other,
            send_sem=cols_send.at[k], recv_sem=cols_recv.at[k],
            device_id=(b, partner_of(g, k)), device_id_type=MESH,
        ).wait_recv()


def border_solve(n_blk, n_grp, term, rhs, inverse):
    link, cols = term.shape
    rows, width = link // n_blk, cols // n_grp
    steps = n_grp.bit_length() - 1
    bf16 = jnp.bfloat16
    halves = [pltpu.VMEM((link, cols >> (k + 1)), bf16) for k in range(steps)]
    slots = pltpu.VMEM((n_blk - 1, rows, width), bf16)
    dma = pltpu.SemaphoreType.DMA
    vmem = pl.BlockSpec(memory_space=pltpu.VMEM)
    return pl.pallas_call(
        functools.partial(border_kernel, n_blk, n_grp),
        out_shape=jax.ShapeDtypeStruct((link, cols), bf16),
        in_specs=[vmem] * 3,
        out_specs=vmem,
        scratch_shapes=[
            halves, list(halves), slots, pltpu.VMEM((link, width), bf16), slots,
            dma((steps,)), dma((steps,)),
            dma((n_blk - 1,)), dma((n_blk - 1,)),
            dma((n_blk - 1,)), dma((n_blk - 1,)),
            dma((n_blk - 1,)), dma((n_blk - 1,)),
            dma((steps,)), dma((steps,)),
        ],
        compiler_params=pltpu.CompilerParams(
            collective_id=0, has_side_effects=True, vmem_limit_bytes=32 * 1024 * 1024
        ),
    )(term, rhs, inverse)


def column_base(n_grp, cols):
    g = lax.axis_index("grp")
    base = 0
    for k in range(n_grp.bit_length() - 1):
        base = base + bit_of(g, k) * (cols >> (k + 1))
    return base


def body(n_blk, n_grp, block_inverse, coupling_in, coupling_out, sensitivities, border_rhs, border_inverse):
    bf16 = jnp.bfloat16
    forward_part = jnp.einsum(
        "bji,bjk->bik", block_inverse, sensitivities, preferred_element_type=jnp.float32
    )
    forward_half = forward_part.astype(bf16)
    row_count = border_inverse.shape[0]
    cols = border_rhs.shape[1]
    first_row = lax.axis_index("blk") * row_count
    rhs = lax.dynamic_slice(
        border_rhs, (first_row, column_base(n_grp, cols)), (row_count, cols // n_grp)
    )
    full_term = jnp.einsum(
        "bnm,bnk->mk", coupling_in, forward_half, preferred_element_type=jnp.float32
    ).astype(bf16)
    full_border = border_solve(n_blk, n_grp, full_term, rhs, border_inverse)
    border_rows = lax.dynamic_slice_in_dim(full_border, first_row, row_count, 0)
    pulled = jnp.einsum(
        "bmn,mk->bnk", coupling_out, full_border, preferred_element_type=jnp.float32
    ).astype(bf16)
    back_term = jnp.einsum(
        "bji,bjk->bik", block_inverse, pulled, preferred_element_type=jnp.float32
    )
    adjoint = (forward_part - back_term).astype(bf16)
    return (adjoint, border_rows)


def solution(mesh):
    in_specs = (
        P(("blk", "grp"), None, None),
        P(("blk", "grp"), None, None),
        P(("blk", "grp"), None, None),
        P(("blk", "grp"), None, None),
        P(),
        P("blk", None),
    )
    out_specs = (P(("blk", "grp"), None, None), P("blk", None))
    run = functools.partial(body, mesh.shape["blk"], mesh.shape["grp"])
    return jax.shard_map(run, mesh=mesh, in_specs=in_specs, out_specs=out_specs, check_vma=False)
```

```python
import functools

import jax
import jax.numpy as jnp
from jax import lax
from jax.experimental import pallas as pl
from jax.experimental.pallas import tpu as pltpu
from jax.sharding import PartitionSpec as P

MESH = pl.DeviceIdType.MESH


def bit_of(index, k):
    return lax.rem(lax.div(index, 1 << k), 2)


def partner_of(index, k):
    return index + (1 - 2 * bit_of(index, k)) * (1 << k)


def border_kernel(
    n_blk, n_grp, parts, flat_ref, rhs_ref, inv_ref, out_ref,
    fold_refs, land_refs, sum_slots, part_ref, part_slots, residual_ref,
    fold_send, fold_recv, sum_send, sum_recv, part_send, part_recv,
    rows_send, rows_recv, cols_send, cols_recv,
):
    b = lax.axis_index("blk")
    g = lax.axis_index("grp")
    link, cols = flat_ref.shape
    rows = link // n_blk
    term_ref = flat_ref.reshape(n_blk, rows, cols)
    piece = rows // parts
    width = cols // n_grp
    steps = n_grp.bit_length() - 1
    f32, bf16 = jnp.float32, jnp.bfloat16
    peers = [lax.rem(b + d, n_blk) for d in range(1, n_blk)]
    origins = [lax.rem(b + n_blk - d, n_blk) for d in range(1, n_blk)]
    partners = [partner_of(g, k) for k in range(steps)]
    bits = [bit_of(g, k) for k in range(steps)]

    barrier = pltpu.get_barrier_semaphore()
    for partner in partners:
        pl.semaphore_signal(barrier, inc=1, device_id=(b, partner), device_id_type=MESH)
    for peer in peers:
        pl.semaphore_signal(barrier, inc=1, device_id=(peer, g), device_id_type=MESH)
    pl.semaphore_wait(barrier, steps + n_blk - 1)

    def rows_of(s):
        return pl.ds(s * piece, piece)

    def columns(index, size, base=0):
        return pl.ds(pl.multiple_of(base + index * size, size), size)

    def send(src, dst, device, send_sem, recv_sem):
        copy = pltpu.make_async_remote_copy(
            src_ref=src, dst_ref=dst, send_sem=send_sem, recv_sem=recv_sem,
            device_id=device, device_id_type=MESH,
        )
        copy.start()
        return copy

    def start_fold(k, s):
        source = term_ref if k == 0 else fold_refs[k - 1]
        half = cols >> (k + 1)
        return send(
            source.at[:, rows_of(s), columns(1 - bits[k], half)],
            land_refs[k].at[:, rows_of(s), :],
            (b, partners[k]), fold_send.at[k, s], fold_recv.at[k, s],
        )

    def start_scatter(src, slots, sends, recvs, s):
        return [
            send(
                src.at[peer, rows_of(s), :], slots.at[i, rows_of(s), :],
                (peer, g), sends.at[i, s], recvs.at[i, s],
            )
            for i, peer in enumerate(peers)
        ]

    def finish_scatter(copies, src, slots, s):
        total = src[b, rows_of(s), :].astype(f32)
        for i, copy in enumerate(copies):
            copy.wait()
            total = total + slots[i, rows_of(s), :].astype(f32)
        return total

    folds = [start_fold(0, s) for s in range(parts)]
    for k in range(steps):
        source = term_ref if k == 0 else fold_refs[k - 1]
        later = []
        for s in range(parts):
            folds[s].wait()
            keep = columns(bits[k], cols >> (k + 1))
            fold_refs[k][:, rows_of(s), :] = (
                source[:, rows_of(s), keep].astype(f32) + land_refs[k][:, rows_of(s), :].astype(f32)
            ).astype(bf16)
            if k + 1 < steps:
                later.append(start_fold(k + 1, s))
            else:
                later.append(start_scatter(fold_refs[k], sum_slots, sum_send, sum_recv, s))
        folds = later
    for s in range(parts):
        total = finish_scatter(folds[s], fold_refs[steps - 1], sum_slots, s)
        residual_ref[rows_of(s), :] = (rhs_ref[rows_of(s), :].astype(f32) - total).astype(bf16)

    part = lax.dot_general(
        inv_ref[...], residual_ref[...], (((0,), (0,)), ((), ())), preferred_element_type=f32
    ).astype(bf16)
    part_ref[...] = part.reshape(part_ref.shape)

    scatters = [
        start_scatter(part_ref, part_slots, part_send, part_recv, s) for s in range(parts)
    ]
    bases = [0]
    for k in range(steps):
        bases.append(bases[k] + bits[k] * (cols >> (k + 1)))
    own = columns(0, width, bases[steps])
    gathers = []
    for s in range(parts):
        total = finish_scatter(scatters[s], part_ref, part_slots, s)
        out_ref[b, rows_of(s), own] = total.astype(bf16)
        place = out_ref.at[b, rows_of(s), own]
        gathers.append([
            send(place, place, (peer, g), rows_send.at[i, s], rows_recv.at[i, s])
            for i, peer in enumerate(peers)
        ])

    def arrived(place, device, send_sem, recv_sem):
        pltpu.make_async_remote_copy(
            src_ref=place, dst_ref=place, send_sem=send_sem, recv_sem=recv_sem,
            device_id=device, device_id_type=MESH,
        ).wait_recv()

    def start_unfold(k, s):
        half = cols >> (k + 1)
        place = out_ref.at[:, rows_of(s), columns(bits[k], half, bases[k])]
        return send(place, place, (b, partners[k]), cols_send.at[k, s], cols_recv.at[k, s])

    unfolds = []
    for s in range(parts):
        for i, origin in enumerate(origins):
            gathers[s][i].wait_send()
            arrived(
                out_ref.at[origin, rows_of(s), own], (peers[i], g),
                rows_send.at[i, s], rows_recv.at[i, s],
            )
        unfolds.append(start_unfold(steps - 1, s))
    for k in reversed(range(steps)):
        half = cols >> (k + 1)
        later = []
        for s in range(parts):
            unfolds[s].wait_send()
            arrived(
                out_ref.at[:, rows_of(s), columns(1 - bits[k], half, bases[k])],
                (b, partners[k]), cols_send.at[k, s], cols_recv.at[k, s],
            )
            if k > 0:
                later.append(start_unfold(k - 1, s))
        unfolds = later


def border_solve(n_blk, n_grp, term, rhs, inverse):
    link, cols = term.shape
    rows, width = link // n_blk, cols // n_grp
    steps = n_grp.bit_length() - 1
    parts = 3 if rows % 48 == 0 else 1
    bf16 = jnp.bfloat16
    halves = [pltpu.VMEM((n_blk, rows, cols >> (k + 1)), bf16) for k in range(steps)]
    slots = pltpu.VMEM((n_blk - 1, rows, width), bf16)
    dma = pltpu.SemaphoreType.DMA
    vmem = pl.BlockSpec(memory_space=pltpu.VMEM)
    out = pl.pallas_call(
        functools.partial(border_kernel, n_blk, n_grp, parts),
        out_shape=jax.ShapeDtypeStruct((n_blk, rows, cols), bf16),
        in_specs=[vmem] * 3,
        out_specs=vmem,
        scratch_shapes=[
            halves, list(halves), slots, pltpu.VMEM((n_blk, rows, width), bf16), slots,
            pltpu.VMEM((rows, width), bf16),
            dma((steps, parts)), dma((steps, parts)),
            dma((n_blk - 1, parts)), dma((n_blk - 1, parts)),
            dma((n_blk - 1, parts)), dma((n_blk - 1, parts)),
            dma((n_blk - 1, parts)), dma((n_blk - 1, parts)),
            dma((steps, parts)), dma((steps, parts)),
        ],
        compiler_params=pltpu.CompilerParams(
            collective_id=0, has_side_effects=True, vmem_limit_bytes=32 * 1024 * 1024
        ),
    )(term, rhs, inverse)
    return out.reshape(link, cols)


def column_base(n_grp, cols):
    g = lax.axis_index("grp")
    base = 0
    for k in range(n_grp.bit_length() - 1):
        base = base + bit_of(g, k) * (cols >> (k + 1))
    return base


def body(n_blk, n_grp, block_inverse, coupling_in, coupling_out, sensitivities, border_rhs, border_inverse):
    bf16 = jnp.bfloat16
    forward_part = jnp.einsum(
        "bji,bjk->bik", block_inverse, sensitivities, preferred_element_type=jnp.float32
    )
    forward_half = forward_part.astype(bf16)
    row_count = border_inverse.shape[0]
    cols = border_rhs.shape[1]
    first_row = lax.axis_index("blk") * row_count
    rhs = lax.dynamic_slice(
        border_rhs, (first_row, column_base(n_grp, cols)), (row_count, cols // n_grp)
    )
    full_term = jnp.einsum(
        "bnm,bnk->mk", coupling_in, forward_half, preferred_element_type=jnp.float32
    ).astype(bf16)
    full_border = border_solve(n_blk, n_grp, full_term, rhs, border_inverse)
    border_rows = lax.dynamic_slice_in_dim(full_border, first_row, row_count, 0)
    pulled = jnp.einsum(
        "bmn,mk->bnk", coupling_out, full_border, preferred_element_type=jnp.float32
    ).astype(bf16)
    back_term = jnp.einsum(
        "bji,bjk->bik", block_inverse, pulled, preferred_element_type=jnp.float32
    )
    adjoint = (forward_part - back_term).astype(bf16)
    return (adjoint, border_rows)


def solution(mesh):
    in_specs = (
        P(("blk", "grp"), None, None),
        P(("blk", "grp"), None, None),
        P(("blk", "grp"), None, None),
        P(("blk", "grp"), None, None),
        P(),
        P("blk", None),
    )
    out_specs = (P(("blk", "grp"), None, None), P("blk", None))
    run = functools.partial(body, mesh.shape["blk"], mesh.shape["grp"])
    return jax.shard_map(run, mesh=mesh, in_specs=in_specs, out_specs=out_specs, check_vma=False)
```

```python
import functools

import jax
import jax.numpy as jnp
from jax import lax
from jax.experimental import pallas as pl
from jax.experimental.pallas import tpu as pltpu
from jax.sharding import PartitionSpec as P

MESH = pl.DeviceIdType.MESH


def bit_of(index, k):
    return lax.rem(lax.div(index, 1 << k), 2)


def partner_of(index, k):
    return index + (1 - 2 * bit_of(index, k)) * (1 << k)


def border_kernel(
    n_blk, n_grp, parts, flat_ref, rhs_hbm, inv_ref, out_ref,
    fold_refs, land_refs, sum_slots, part_ref, part_slots, residual_ref, rhs_ref, rhs_sem,
    fold_send, fold_recv, sum_send, sum_recv, part_send, part_recv,
    rows_send, rows_recv, cols_send, cols_recv,
):
    b = lax.axis_index("blk")
    g = lax.axis_index("grp")
    link, cols = flat_ref.shape
    rows = link // n_blk
    term_ref = flat_ref.reshape(n_blk, rows, cols)
    piece = rows // parts
    width = cols // n_grp
    steps = n_grp.bit_length() - 1
    f32, bf16 = jnp.float32, jnp.bfloat16
    peers = [lax.rem(b + d, n_blk) for d in range(1, n_blk)]
    origins = [lax.rem(b + n_blk - d, n_blk) for d in range(1, n_blk)]
    partners = [partner_of(g, k) for k in range(steps)]
    bits = [bit_of(g, k) for k in range(steps)]

    bases = [0]
    for k in range(steps):
        bases.append(bases[k] + bits[k] * (cols >> (k + 1)))
    fetch = pltpu.make_async_copy(
        rhs_hbm.at[pl.ds(pl.multiple_of(b * rows, rows), rows),
                   pl.ds(pl.multiple_of(bases[steps], width), width)],
        rhs_ref, rhs_sem,
    )
    fetch.start()

    barrier = pltpu.get_barrier_semaphore()
    for partner in partners:
        pl.semaphore_signal(barrier, inc=1, device_id=(b, partner), device_id_type=MESH)
    for peer in peers:
        pl.semaphore_signal(barrier, inc=1, device_id=(peer, g), device_id_type=MESH)
    pl.semaphore_wait(barrier, steps + n_blk - 1)

    def rows_of(s):
        return pl.ds(s * piece, piece)

    def columns(index, size, base=0):
        return pl.ds(pl.multiple_of(base + index * size, size), size)

    def send(src, dst, device, send_sem, recv_sem):
        copy = pltpu.make_async_remote_copy(
            src_ref=src, dst_ref=dst, send_sem=send_sem, recv_sem=recv_sem,
            device_id=device, device_id_type=MESH,
        )
        copy.start()
        return copy

    def start_fold(k, s):
        source = term_ref if k == 0 else fold_refs[k - 1]
        half = cols >> (k + 1)
        return send(
            source.at[:, rows_of(s), columns(1 - bits[k], half)],
            land_refs[k].at[:, rows_of(s), :],
            (b, partners[k]), fold_send.at[k, s], fold_recv.at[k, s],
        )

    def start_scatter(src, slots, sends, recvs, s):
        return [
            send(
                src.at[peer, rows_of(s), :], slots.at[i, rows_of(s), :],
                (peer, g), sends.at[i, s], recvs.at[i, s],
            )
            for i, peer in enumerate(peers)
        ]

    def finish_scatter(copies, src, slots, s):
        total = src[b, rows_of(s), :].astype(f32)
        for i, copy in enumerate(copies):
            copy.wait()
            total = total + slots[i, rows_of(s), :].astype(f32)
        return total

    folds = [start_fold(0, s) for s in range(parts)]
    for k in range(steps):
        source = term_ref if k == 0 else fold_refs[k - 1]
        later = []
        for s in range(parts):
            folds[s].wait()
            keep = columns(bits[k], cols >> (k + 1))
            fold_refs[k][:, rows_of(s), :] = (
                source[:, rows_of(s), keep].astype(f32) + land_refs[k][:, rows_of(s), :].astype(f32)
            ).astype(bf16)
            if k + 1 < steps:
                later.append(start_fold(k + 1, s))
            else:
                later.append(start_scatter(fold_refs[k], sum_slots, sum_send, sum_recv, s))
        folds = later
    fetch.wait()
    for s in range(parts):
        total = finish_scatter(folds[s], fold_refs[steps - 1], sum_slots, s)
        residual_ref[rows_of(s), :] = (rhs_ref[rows_of(s), :].astype(f32) - total).astype(bf16)

    part = lax.dot_general(
        inv_ref[...], residual_ref[...], (((0,), (0,)), ((), ())), preferred_element_type=f32
    ).astype(bf16)
    part_ref[...] = part.reshape(part_ref.shape)

    scatters = [
        start_scatter(part_ref, part_slots, part_send, part_recv, s) for s in range(parts)
    ]
    own = columns(0, width, bases[steps])
    gathers = []
    for s in range(parts):
        total = finish_scatter(scatters[s], part_ref, part_slots, s)
        out_ref[b, rows_of(s), own] = total.astype(bf16)
        place = out_ref.at[b, rows_of(s), own]
        gathers.append([
            send(place, place, (peer, g), rows_send.at[i, s], rows_recv.at[i, s])
            for i, peer in enumerate(peers)
        ])

    def arrived(place, device, send_sem, recv_sem):
        pltpu.make_async_remote_copy(
            src_ref=place, dst_ref=place, send_sem=send_sem, recv_sem=recv_sem,
            device_id=device, device_id_type=MESH,
        ).wait_recv()

    def start_unfold(k, s):
        half = cols >> (k + 1)
        place = out_ref.at[:, rows_of(s), columns(bits[k], half, bases[k])]
        return send(place, place, (b, partners[k]), cols_send.at[k, s], cols_recv.at[k, s])

    unfolds = []
    for s in range(parts):
        for i, origin in enumerate(origins):
            gathers[s][i].wait_send()
            arrived(
                out_ref.at[origin, rows_of(s), own], (peers[i], g),
                rows_send.at[i, s], rows_recv.at[i, s],
            )
        unfolds.append(start_unfold(steps - 1, s))
    for k in reversed(range(steps)):
        half = cols >> (k + 1)
        later = []
        for s in range(parts):
            unfolds[s].wait_send()
            arrived(
                out_ref.at[:, rows_of(s), columns(1 - bits[k], half, bases[k])],
                (b, partners[k]), cols_send.at[k, s], cols_recv.at[k, s],
            )
            if k > 0:
                later.append(start_unfold(k - 1, s))
        unfolds = later


def border_solve(n_blk, n_grp, term, rhs, inverse):
    link, cols = term.shape
    rows, width = link // n_blk, cols // n_grp
    steps = n_grp.bit_length() - 1
    parts = max(p for p in (1, 2, 3) if rows % (16 * p) == 0)
    bf16 = jnp.bfloat16
    halves = [pltpu.VMEM((n_blk, rows, cols >> (k + 1)), bf16) for k in range(steps)]
    slots = pltpu.VMEM((n_blk - 1, rows, width), bf16)
    dma = pltpu.SemaphoreType.DMA
    vmem = pl.BlockSpec(memory_space=pltpu.VMEM)
    out = pl.pallas_call(
        functools.partial(border_kernel, n_blk, n_grp, parts),
        out_shape=jax.ShapeDtypeStruct((n_blk, rows, cols), bf16),
        in_specs=[vmem, pl.BlockSpec(memory_space=pl.ANY), vmem],
        out_specs=vmem,
        scratch_shapes=[
            halves, list(halves), slots, pltpu.VMEM((n_blk, rows, width), bf16), slots,
            pltpu.VMEM((rows, width), bf16), pltpu.VMEM((rows, width), bf16), dma,
            dma((steps, parts)), dma((steps, parts)),
            dma((n_blk - 1, parts)), dma((n_blk - 1, parts)),
            dma((n_blk - 1, parts)), dma((n_blk - 1, parts)),
            dma((n_blk - 1, parts)), dma((n_blk - 1, parts)),
            dma((steps, parts)), dma((steps, parts)),
        ],
        compiler_params=pltpu.CompilerParams(
            collective_id=0, has_side_effects=True, vmem_limit_bytes=12 * 1024 * 1024
        ),
    )(term, rhs, inverse)
    return out.reshape(link, cols)


def body(n_blk, n_grp, block_inverse, coupling_in, coupling_out, sensitivities, border_rhs, border_inverse):
    bf16 = jnp.bfloat16
    forward_part = jnp.einsum(
        "bji,bjk->bik", block_inverse, sensitivities, preferred_element_type=jnp.float32
    )
    forward_half = forward_part.astype(bf16)
    row_count = border_inverse.shape[0]
    first_row = lax.axis_index("blk") * row_count
    full_term = jnp.einsum(
        "bnm,bnk->mk", coupling_in, forward_half, preferred_element_type=jnp.float32
    ).astype(bf16)
    full_border = border_solve(n_blk, n_grp, full_term, border_rhs, border_inverse)
    border_rows = lax.dynamic_slice_in_dim(full_border, first_row, row_count, 0)
    pulled = jnp.einsum(
        "bmn,mk->bnk", coupling_out, full_border, preferred_element_type=jnp.float32
    ).astype(bf16)
    pulled = lax.optimization_barrier(pulled)
    back_term = jnp.einsum(
        "bji,bjk->bik", block_inverse, pulled, preferred_element_type=jnp.float32
    )
    adjoint = (forward_part - back_term).astype(bf16)
    return (adjoint, border_rows)


def solution(mesh):
    in_specs = (
        P(("blk", "grp"), None, None),
        P(("blk", "grp"), None, None),
        P(("blk", "grp"), None, None),
        P(("blk", "grp"), None, None),
        P(),
        P("blk", None),
    )
    out_specs = (P(("blk", "grp"), None, None), P("blk", None))
    run = functools.partial(body, mesh.shape["blk"], mesh.shape["grp"])
    return jax.shard_map(run, mesh=mesh, in_specs=in_specs, out_specs=out_specs, check_vma=False)
```

```python
import functools

import jax
import jax.numpy as jnp
from jax import lax
from jax.experimental import pallas as pl
from jax.experimental.pallas import tpu as pltpu
from jax.sharding import PartitionSpec as P

MESH = pl.DeviceIdType.MESH


def bit_of(index, k):
    return lax.rem(lax.div(index, 1 << k), 2)


def partner_of(index, k):
    return index + (1 - 2 * bit_of(index, k)) * (1 << k)


def border_kernel(
    n_blk, n_grp, parts, flat_ref, rhs_hbm, inv_ref, out_ref,
    fold_refs, land_refs, sum_slots, part_ref, pair_land, pair_ref, part_slots, residual_ref, rhs_ref, rhs_sem,
    fold_send, fold_recv, sum_send, sum_recv, part_send, part_recv,
    pair_send, pair_recv, rows_send, rows_recv, mate_send, mate_recv, cols_send, cols_recv,
):
    b = lax.axis_index("blk")
    g = lax.axis_index("grp")
    link, cols = flat_ref.shape
    rows = link // n_blk
    term_ref = flat_ref.reshape(n_blk, rows, cols)
    piece = rows // parts
    width = cols // n_grp
    steps = n_grp.bit_length() - 1
    f32, bf16 = jnp.float32, jnp.bfloat16
    peers = [lax.rem(b + d, n_blk) for d in range(1, n_blk)]
    pairs = n_blk // 2
    side, pair = lax.rem(b, 2), lax.div(b, 2)
    mate = b + 1 - 2 * side
    near = [lax.rem(pair + d, pairs) for d in range(1, pairs)]
    origins = [lax.rem(pair + pairs - d, pairs) for d in range(1, pairs)]
    partners = [partner_of(g, k) for k in range(steps)]
    bits = [bit_of(g, k) for k in range(steps)]

    bases = [0]
    for k in range(steps):
        bases.append(bases[k] + bits[k] * (cols >> (k + 1)))
    fetch = pltpu.make_async_copy(
        rhs_hbm.at[pl.ds(pl.multiple_of(b * rows, rows), rows),
                   pl.ds(pl.multiple_of(bases[steps], width), width)],
        rhs_ref, rhs_sem,
    )
    fetch.start()

    barrier = pltpu.get_barrier_semaphore()
    for partner in partners:
        pl.semaphore_signal(barrier, inc=1, device_id=(b, partner), device_id_type=MESH)
    for peer in peers:
        pl.semaphore_signal(barrier, inc=1, device_id=(peer, g), device_id_type=MESH)
    pl.semaphore_wait(barrier, steps + n_blk - 1)

    def rows_of(s):
        return pl.ds(s * piece, piece)

    def columns(index, size, base=0):
        return pl.ds(pl.multiple_of(base + index * size, size), size)

    def send(src, dst, device, send_sem, recv_sem):
        copy = pltpu.make_async_remote_copy(
            src_ref=src, dst_ref=dst, send_sem=send_sem, recv_sem=recv_sem,
            device_id=device, device_id_type=MESH,
        )
        copy.start()
        return copy

    def start_fold(k, s):
        source = term_ref if k == 0 else fold_refs[k - 1]
        half = cols >> (k + 1)
        return send(
            source.at[:, rows_of(s), columns(1 - bits[k], half)],
            land_refs[k].at[:, rows_of(s), :],
            (b, partners[k]), fold_send.at[k, s], fold_recv.at[k, s],
        )

    def start_scatter(src, slots, sends, recvs, s, places, owners):
        return [
            send(
                src.at[place, rows_of(s), :], slots.at[i, rows_of(s), :],
                (owner, g), sends.at[i, s], recvs.at[i, s],
            )
            for i, (place, owner) in enumerate(zip(places, owners))
        ]

    def finish_scatter(copies, src, slots, s, place):
        total = src[place, rows_of(s), :].astype(f32)
        for i, copy in enumerate(copies):
            copy.wait()
            total = total + slots[i, rows_of(s), :].astype(f32)
        return total

    folds = [start_fold(0, s) for s in range(parts)]
    for k in range(steps):
        source = term_ref if k == 0 else fold_refs[k - 1]
        later = []
        for s in range(parts):
            folds[s].wait()
            keep = columns(bits[k], cols >> (k + 1))
            fold_refs[k][:, rows_of(s), :] = (
                source[:, rows_of(s), keep].astype(f32) + land_refs[k][:, rows_of(s), :].astype(f32)
            ).astype(bf16)
            if k + 1 < steps:
                later.append(start_fold(k + 1, s))
            else:
                later.append(start_scatter(
                    fold_refs[k], sum_slots, sum_send, sum_recv, s, peers, peers
                ))
        folds = later
    fetch.wait()
    for s in range(parts):
        total = finish_scatter(folds[s], fold_refs[steps - 1], sum_slots, s, b)
        residual_ref[rows_of(s), :] = (rhs_ref[rows_of(s), :].astype(f32) - total).astype(bf16)

    part = lax.dot_general(
        inv_ref[...], residual_ref[...], (((0,), (0,)), ((), ())), preferred_element_type=f32
    ).astype(bf16)
    part_ref[...] = part.reshape(part_ref.shape)

    owners = [place * 2 + side for place in near]
    swaps = [
        send(
            part_ref.at[:, 1 - side, rows_of(s), :], pair_land.at[:, rows_of(s), :],
            (mate, g), pair_send.at[s], pair_recv.at[s],
        )
        for s in range(parts)
    ]
    scatters = []
    for s in range(parts):
        swaps[s].wait()
        pair_ref[:, rows_of(s), :] = (
            part_ref[:, side, rows_of(s), :].astype(f32) + pair_land[:, rows_of(s), :].astype(f32)
        ).astype(bf16)
        scatters.append(start_scatter(
            pair_ref, part_slots, part_send, part_recv, s, near, owners
        ))
    own = columns(0, width, bases[steps])
    gathers = []
    for s in range(parts):
        total = finish_scatter(scatters[s], pair_ref, part_slots, s, pair)
        out_ref[pair, side, rows_of(s), own] = total.astype(bf16)
        place = out_ref.at[pair, side, rows_of(s), own]
        gathers.append([
            send(place, place, (owner, g), rows_send.at[i, s], rows_recv.at[i, s])
            for i, owner in enumerate(owners)
        ])

    def arrived(place, device, send_sem, recv_sem):
        pltpu.make_async_remote_copy(
            src_ref=place, dst_ref=place, send_sem=send_sem, recv_sem=recv_sem,
            device_id=device, device_id_type=MESH,
        ).wait_recv()

    def start_unfold(k, s):
        half = cols >> (k + 1)
        place = out_ref.at[:, :, rows_of(s), columns(bits[k], half, bases[k])]
        return send(place, place, (b, partners[k]), cols_send.at[k, s], cols_recv.at[k, s])

    swaps = []
    for s in range(parts):
        for i, origin in enumerate(origins):
            gathers[s][i].wait_send()
            arrived(
                out_ref.at[origin, side, rows_of(s), own], (owners[i], g),
                rows_send.at[i, s], rows_recv.at[i, s],
            )
        place = out_ref.at[:, side, rows_of(s), own]
        swaps.append(send(place, place, (mate, g), mate_send.at[s], mate_recv.at[s]))
    unfolds = []
    for s in range(parts):
        swaps[s].wait_send()
        arrived(
            out_ref.at[:, 1 - side, rows_of(s), own], (mate, g),
            mate_send.at[s], mate_recv.at[s],
        )
        unfolds.append(start_unfold(steps - 1, s))
    for k in reversed(range(steps)):
        half = cols >> (k + 1)
        later = []
        for s in range(parts):
            unfolds[s].wait_send()
            arrived(
                out_ref.at[:, :, rows_of(s), columns(1 - bits[k], half, bases[k])],
                (b, partners[k]), cols_send.at[k, s], cols_recv.at[k, s],
            )
            if k > 0:
                later.append(start_unfold(k - 1, s))
        unfolds = later


def border_solve(n_blk, n_grp, term, rhs, inverse):
    link, cols = term.shape
    rows, width = link // n_blk, cols // n_grp
    steps = n_grp.bit_length() - 1
    parts = max(p for p in (1, 2, 3, 4) if rows % (16 * p) == 0)
    bf16 = jnp.bfloat16
    halves = [pltpu.VMEM((n_blk, rows, cols >> (k + 1)), bf16) for k in range(steps)]
    slots = pltpu.VMEM((n_blk - 1, rows, width), bf16)
    dma = pltpu.SemaphoreType.DMA
    vmem = pl.BlockSpec(memory_space=pltpu.VMEM)
    out = pl.pallas_call(
        functools.partial(border_kernel, n_blk, n_grp, parts),
        out_shape=jax.ShapeDtypeStruct((n_blk // 2, 2, rows, cols), bf16),
        in_specs=[vmem, pl.BlockSpec(memory_space=pl.ANY), vmem],
        out_specs=vmem,
        scratch_shapes=[
            halves, list(halves), slots, pltpu.VMEM((n_blk // 2, 2, rows, width), bf16),
            pltpu.VMEM((n_blk // 2, rows, width), bf16), pltpu.VMEM((n_blk // 2, rows, width), bf16),
            pltpu.VMEM((n_blk // 2 - 1, rows, width), bf16),
            pltpu.VMEM((rows, width), bf16), pltpu.VMEM((rows, width), bf16), dma,
            dma((steps, parts)), dma((steps, parts)),
            dma((n_blk - 1, parts)), dma((n_blk - 1, parts)),
            dma((n_blk // 2 - 1, parts)), dma((n_blk // 2 - 1, parts)),
            dma((parts,)), dma((parts,)),
            dma((n_blk // 2 - 1, parts)), dma((n_blk // 2 - 1, parts)),
            dma((parts,)), dma((parts,)),
            dma((steps, parts)), dma((steps, parts)),
        ],
        compiler_params=pltpu.CompilerParams(
            collective_id=0, has_side_effects=True, vmem_limit_bytes=12 * 1024 * 1024
        ),
    )(term, rhs, inverse)
    return out.reshape(link, cols)


def body(n_blk, n_grp, block_inverse, coupling_in, coupling_out, sensitivities, border_rhs, border_inverse):
    bf16 = jnp.bfloat16
    forward_part = jnp.einsum(
        "bji,bjk->bik", block_inverse, sensitivities, preferred_element_type=jnp.float32
    )
    forward_half = forward_part.astype(bf16)
    row_count = border_inverse.shape[0]
    first_row = lax.axis_index("blk") * row_count
    full_term = jnp.einsum(
        "bnm,bnk->mk", coupling_in, forward_half, preferred_element_type=jnp.float32
    ).astype(bf16)
    full_border = border_solve(n_blk, n_grp, full_term, border_rhs, border_inverse)
    border_rows = lax.dynamic_slice_in_dim(full_border, first_row, row_count, 0)
    pulled = jnp.einsum(
        "bmn,mk->bnk", coupling_out, full_border, preferred_element_type=jnp.float32
    ).astype(bf16)
    pulled = lax.optimization_barrier(pulled)
    back_term = jnp.einsum(
        "bji,bjk->bik", block_inverse, pulled, preferred_element_type=jnp.float32
    )
    adjoint = (forward_part - back_term).astype(bf16)
    return (adjoint, border_rows)


def solution(mesh):
    in_specs = (
        P(("blk", "grp"), None, None),
        P(("blk", "grp"), None, None),
        P(("blk", "grp"), None, None),
        P(("blk", "grp"), None, None),
        P(),
        P("blk", None),
    )
    out_specs = (P(("blk", "grp"), None, None), P("blk", None))
    run = functools.partial(body, mesh.shape["blk"], mesh.shape["grp"])
    return jax.shard_map(run, mesh=mesh, in_specs=in_specs, out_specs=out_specs, check_vma=False)
```
